512 devices in a mesh: sess: 32 (over z_hi, x, core), ctx: 16 (over y, z_lo).
Axes of the slice: x: 4, y: 4, z: 16 (z_hi: 4, z_lo: 4; z = z_hi * 4 + z_lo), core: 2. Of those that a mesh axis runs over, the one named last changes fastest.
Arguments:
- page_store: bfloat16 [32, 16, 32, 2, 16, 2, 512], P('sess', 'ctx'), may hold values from -6 to 6
- page_holder: int32 [32, 128, 1], P('sess', 'ctx'), may hold values from 0 to 31; in each aligned block of 8 rows (0 to 7, 8 to 15, ..., all dimensions but the last counted through in order) at most 2 rows name the same one
- history_length: int32 [32], P('sess'), may hold values from 256 to 2048
- old_offset: int32 [32], P('sess'), may hold values from 0 to 1023
- turn_query: bfloat16 [32, 256, 4096], P('sess', 'ctx'), may hold values from -128 to 128
- turn_key: bfloat16 [32, 256, 512], P('sess', 'ctx'), may hold values from -6 to 6
- turn_value: bfloat16 [32, 256, 512], P('sess', 'ctx'), may hold values from -6 to 6
Outputs:
- attended: bfloat16 [32, 256, 4096], P('sess', 'ctx')
The draws below stay inside these ranges and needn't reach their ends.
Inputs may be any that keep to these rules, and one draw needn't show every extreme that they name: `page_holder`: among the 8 pages of one device's block, at most 2 name the same holder, and the k-th of them (in page order) lies in that holder's slot k for the session.
All inputs are finite; a program needn't handle non-finite values.
Results may differ from the reference program's by a relative error of at most 0.011.
Values may be sent and summed in bfloat16 or wider, within the bound.
A program may use at most 64 MiB of HBM per device.

```python
import math
import jax
import jax.numpy as jnp
import numpy as np
from jax import lax

KVH = 4
GROUP = 8
HD = 128
PAGE = 16
PPD = 8
SESSIONS = 32
LOOP = 16
CAP = 2
HIST = 2048
TURN = 256
PAGES = 128


def draw_history_length(key, part):
    key = jax.random.fold_in(key, 11)
    spread = jax.random.randint(key, (SESSIONS,), 0, 101)
    lengths = HIST // 8 + (HIST - HIST // 8) * spread * spread // 10000
    chosen = jax.random.randint(jax.random.fold_in(key, 1), (), 0, SESSIONS)
    return jnp.where(jnp.arange(SESSIONS) == chosen, HIST, lengths).astype(jnp.int32)


def draw_turn_query(key, part):
    key = jax.random.fold_in(key, 23)
    shape = (SESSIONS, TURN, KVH * GROUP * HD)
    return (jax.random.truncated_normal(key, -4.0, 4.0, shape, jnp.float32) * 2.5).astype(jnp.bfloat16)


def plant(drawn, own_key, least, top_value):
    place = [jax.random.randint(jax.random.fold_in(own_key, axis), (), 0, length) for axis, length in enumerate(drawn.shape)]
    main_axis = drawn.shape.index(max(drawn.shape))
    beside = place[:main_axis] + [(place[main_axis] + 1) % drawn.shape[main_axis]] + place[main_axis + 1:]
    return drawn.at[tuple(place)].set(least).at[tuple(beside)].set(top_value)


def block_levels(stream_key, dims, shards, low, top_value):
    def one(dim, parts):
        heights = jax.random.uniform(jax.random.fold_in(jax.random.fold_in(stream_key, 6), dim), (parts,), jnp.float32, low / len(shards), top_value / len(shards))
        return jnp.repeat(jnp.exp(heights), dims[dim] // parts).reshape((-1,) + (1,) * (len(dims) - dim - 1))

    level = one(*shards[0])
    for cut in shards[1:]:
        level = level * one(*cut)
    return level


def deal_out(stream_key, own, number, rows, count, top, bound, skew):
    ranking = jax.random.permutation(stream_key, count)
    crowded, common = load_shares(count, rows * top, bound, skew, True), load_shares(count, rows * top, bound, skew, False)
    places = jnp.arange(count)

    def named(tallies, turn):
        used = int((tallies > 0).sum())
        fixed = max(1, used // 4)
        shifted = fixed + (places - fixed + turn * (used - fixed)) % max(1, count - fixed)
        return jnp.zeros((count,), jnp.int32).at[ranking[jnp.where(places < fixed, places, shifted)]].set(jnp.asarray(tallies, jnp.int32))

    tallies = jnp.where(number % 4 == 0, named(crowded, number // 4), named(common, number - number // 4 - 1))
    mixed = jax.random.permutation(jax.random.fold_in(own, 3), count)
    source_of, receiver = mixed[0:count // 2 * 2:2], mixed[1:count // 2 * 2:2]
    slack = jnp.minimum(tallies[source_of] - 1, bound - tallies[receiver]) // 2
    slack = jnp.where((source_of == ranking[0]) | (receiver == ranking[0]) | (tallies[receiver] == 0), 0, jnp.maximum(slack, 0))
    shifted = jax.random.randint(jax.random.fold_in(own, 4), (count // 2,), 0, 1 << 20) % (slack + 1)
    tallies = tallies.at[source_of].add(-shifted).at[receiver].add(shifted)
    labels = jnp.searchsorted(jnp.cumsum(tallies), jnp.arange(rows * top), side="right").astype(jnp.int32)
    listing = labels.reshape(top, rows).T
    listing = listing[jax.random.permutation(jax.random.fold_in(own, 1), rows)]
    turn = jax.random.randint(jax.random.fold_in(own, 2), (rows, 1), 0, top)
    return jnp.take_along_axis(listing, (jnp.arange(top)[None, :] + turn) % top, axis=1)


def load_shares(amount, total, most, skew, full):
    portions = [(1 << 20) // math.isqrt(standing ** skew) + 1 for standing in range(1, amount + 1)]
    largest = most if full else min(most, max(-(-total // amount), total * portions[0] // sum(portions)))
    least = 1 if total - largest >= amount - 1 else 0
    counts, surplus = [largest] + [least] * (amount - 1), total - largest - least * (amount - 1)
    while surplus > 0:
        movable = [i for i in range(1, amount) if counts[i] < largest] or [i for i in range(1, amount) if counts[i] < most]
        mass, remaining = sum([portions[i] for i in movable]), surplus
        for i in movable:
            addition = min(most - counts[i], max(1, remaining * portions[i] // mass), surplus)
            counts[i] = counts[i] + addition
            surplus = surplus - addition
    return np.array(counts)


def gaussian(stream_key, extent, scale, bound, split=(), kind=jnp.bfloat16):
    factor_of = block_levels(stream_key, extent, split, -0.22, 0.18) if split else 1.0
    result = jax.random.normal(stream_key, extent, jnp.float32) * scale * factor_of
    return jnp.minimum(jnp.maximum(result, -bound), bound).astype(kind)


def setup_inputs(seed: int = 0) -> dict:
    key_of = jax.random.split(jax.random.key(seed), 8)
    page_store = gaussian(key_of[0], (SESSIONS, LOOP, SESSIONS, CAP, PAGE, 2, KVH * HD), 1.0, 6.0, ((0, 32), (1, 16)))
    page_holder_keys = jax.random.split(jax.random.fold_in(key_of[1], 1), SESSIONS * PAGES // PPD)
    page_holder_turns = jax.random.permutation(jax.random.fold_in(key_of[1], 3), SESSIONS * PAGES // PPD)
    page_holder = jax.vmap(lambda own, number: deal_out(jax.random.fold_in(key_of[1], 2), own, number, PPD, SESSIONS, 1, CAP, 0))(page_holder_keys, page_holder_turns).reshape((SESSIONS, PAGES, 1))
    history_length = draw_history_length(jax.random.fold_in(key_of[7], 71), 0)
    old_offset = plant(jax.random.randint(key_of[3], (SESSIONS,), 0, 1024), jax.random.fold_in(key_of[3], 1), 0, 1023).astype(jnp.int32)
    turn_query = draw_turn_query(jax.random.fold_in(key_of[7], 71), 0)
    turn_key = gaussian(key_of[5], (SESSIONS, TURN, KVH * HD), 1.0, 6.0, ((0, 32), (1, 16)))
    turn_value = gaussian(key_of[6], (SESSIONS, TURN, KVH * HD), 1.0, 6.0, ((0, 32), (1, 16)))
    return {"page_store": page_store, "page_holder": page_holder, "history_length": history_length, "old_offset": old_offset, "turn_query": turn_query, "turn_key": turn_key, "turn_value": turn_value}


ROPE_BASE = 1000000.0
MASKED = -1.0e30


def rotate(values, positions):
    middle = values.shape[-1] // 2
    exponent = jnp.arange(middle, dtype=jnp.float32) * (2.0 / values.shape[-1])
    frequency = jnp.power(jnp.float32(ROPE_BASE), -exponent)
    angles = positions.astype(jnp.float32)[:, None] * frequency[None, :]
    cosine = jnp.cos(angles)[:, None, :]
    sine_part = jnp.sin(angles)[:, None, :]
    leading = values[..., :middle]
    trailing = values[..., middle:]
    return jnp.concatenate([leading * cosine - trailing * sine_part, trailing * cosine + leading * sine_part], axis=-1)


def page_ranks(holders):
    pages_count = holders.shape[-1]
    matches = holders[..., :, None] == holders[..., None, :]
    earlier = jnp.arange(pages_count)[:, None] > jnp.arange(pages_count)[None, :]
    return jnp.sum((matches & earlier).astype(jnp.int32), axis=-1)


def reference(page_store, page_holder, history_length, old_offset, turn_query, turn_key, turn_value):
    def one_session(index):
        holders = lax.dynamic_index_in_dim(page_holder, index, 0, keepdims=False)[:, 0].reshape(LOOP, PPD)
        ranks = page_ranks(holders)
        members = jnp.arange(LOOP, dtype=jnp.int32)[:, None]
        chosen = page_store[holders, members, index, ranks]
        history = chosen.reshape(HIST, 2, KVH, HD)
        length = history_length[index]
        offset_shift = -old_offset[index]
        keys_past = rotate(history[:, 0].astype(jnp.float32), jnp.full((HIST,), offset_shift, jnp.int32)).astype(jnp.bfloat16)
        places = length + jnp.arange(TURN, dtype=jnp.int32)
        queries = rotate(turn_query[index].astype(jnp.float32).reshape(TURN, KVH * GROUP, HD), places).astype(jnp.bfloat16)
        keys_new = rotate(turn_key[index].astype(jnp.float32).reshape(TURN, KVH, HD), places).astype(jnp.bfloat16)
        keys_all = lax.optimization_barrier(jnp.concatenate([keys_past, keys_new], 0)).astype(jnp.float32)
        values_all = jnp.concatenate([history[:, 1], turn_value[index].reshape(TURN, KVH, HD)], 0).astype(jnp.float32)
        grouped = lax.optimization_barrier(queries).astype(jnp.float32).reshape(TURN, KVH, GROUP, HD)
        scores = jnp.einsum("tkgd,skd->kgts", grouped, keys_all) * (HD ** -0.5)
        key_rows = jnp.arange(HIST + TURN, dtype=jnp.int32)[None, :]
        query_rows = jnp.arange(TURN, dtype=jnp.int32)[:, None]
        usable = jnp.where(key_rows < HIST, key_rows < length, key_rows - HIST <= query_rows)
        masked = jnp.where(usable, scores, MASKED)
        highest = jnp.max(masked, axis=-1, keepdims=True)
        weights = jnp.where(usable, jnp.exp(masked - highest), 0.0)
        total = jnp.sum(weights, axis=-1)
        rounded = lax.optimization_barrier(weights.astype(jnp.bfloat16)).astype(jnp.float32)
        summed = jnp.einsum("kgts,skd->tkgd", rounded, values_all)
        mixed = summed / jnp.transpose(total, (2, 0, 1))[..., None]
        return mixed.reshape(TURN, KVH * GROUP * HD).astype(jnp.bfloat16)

    return lax.map(one_session, jnp.arange(SESSIONS, dtype=jnp.int32))
```

```python
import functools

import jax
import jax.numpy as jnp
import numpy as np
from jax import lax
from jax.experimental import pallas as pl
from jax.experimental.pallas import tpu as pltpu
from jax.sharding import PartitionSpec as P

MESH = pl.DeviceIdType.MESH
KVH = 4
GROUP = 8
HD = 128
PAGE = 16
PPD = 8
ROPE_BASE = 1000000.0
MASKED = -1e30
SCALE2 = HD ** (-0.5) * 1.4426950408889634
NH = 2
T = PAGE // NH
ROWS = PPD * T
HALF = PPD // 2


def turned(v, cosine, sine):
    return v * cosine + pltpu.roll(v, HD // 2, 1) * sine


def wait_for(view, sem):
    pltpu.make_async_copy(view, view, sem).wait()


def kernel(hold_ref, length_ref, offset_ref, freq_ref, store, q_ref, k_ref, v_ref, out_ref, *scratch):
    rx = [scratch[r * NH : (r + 1) * NH] for r in range(4)]
    (
        s1, s2, s3, via_a, via_b, left, right, ks, ka, ns, na, qs, qa, qm, os_, oa, hv, hs,
        acc, top, tot, x_send, x_recv, z_send, z_recv, c_send, c_recv, h_sem, l_sem,
    ) = scratch[4 * NH :]
    sess = lax.axis_index("sess")
    ctx = lax.axis_index("ctx")
    z, eighth = sess // 8, sess % 8
    x, core = eighth // 2, eighth % 2
    y, low = ctx // 4, ctx % 4

    def plane(step):
        return lax.rem(z + step, 4)

    def at_plane(step):
        return (plane(step) * 8 + eighth, ctx)

    def mate(dx, dc):
        return lax.rem(x + dx, 4) * 2 + lax.rem(core + dc, 2)

    def at_low(step):
        return (sess, y * 4 + lax.rem(low + step, 4))

    def at_y(step):
        return (sess, lax.rem(y + step, 4) * 4 + low)

    mates = [(dx, dc) for dx in (2, 1, 3, 0) for dc in (0, 1) if (dx, dc) != (0, 0)]

    barrier = pltpu.get_barrier_semaphore()
    others = [(z * 8 + mate(*m), ctx) for m in mates]
    others += [at_plane(i) for i in (1, 2, 3)] + [at_low(i) for i in (1, 2, 3)] + [at_y(i) for i in (1, 2, 3)]
    for other in others:
        pl.semaphore_signal(barrier, inc=1, device_id=other, device_id_type=MESH)

    names = []
    for p in range(PPD):
        rank = jnp.int32(0)
        for e in range(p):
            rank = rank + jnp.where(hold_ref[0, e, 0] == hold_ref[0, p, 0], 1, 0).astype(jnp.int32)
        names.append(hold_ref[0, p, 0] * 2 + rank)
    row = lax.broadcasted_iota(jnp.int32, (PPD, 128), 0)
    table = jnp.zeros((PPD, 128), jnp.int32)
    for p in range(PPD):
        table = jnp.where(row == p, names[p], table)
    hv[z] = table

    pl.semaphore_wait(barrier, len(others))

    def send(src, dst, send_sem, recv_sem, to):
        pltpu.make_async_remote_copy(
            src_ref=src, dst_ref=dst, send_sem=send_sem, recv_sem=recv_sem, device_id=to, device_id_type=MESH
        ).start()

    for i in (1, 2, 3):
        send(hv.at[z], hv.at[z], h_sem.at[0], h_sem.at[1], at_plane(i))

    order = [(2, h) for h in range(NH)] + [(r, h) for h in range(NH) for r in (1, 3)] + [(0, h) for h in range(NH)]
    for r, h in order:
        mine = pl.ds(eighth * 2, 2)
        tokens = pl.ds(h * T, T)
        for m in mates:
            other = mate(*m)
            send(
                store.at[0, 0, plane(r) * 8 + other, :, tokens], rx[r][h].at[mine],
                x_send.at[r, h], x_recv.at[r, h], (z * 8 + other, ctx),
            )
        pltpu.make_async_copy(
            store.at[0, 0, plane(r) * 8 + eighth, :, tokens], rx[r][h].at[mine], x_recv.at[r, h]
        ).start()

    freq = freq_ref[0:1, :]
    sign = freq_ref[1:2, :]
    places = length_ref[0] + ctx * 16 + lax.broadcasted_iota(jnp.int32, (16, HD), 0)
    angles = places.astype(jnp.float32) * freq
    cosine, sine = jnp.cos(angles), jnp.sin(angles) * sign
    for head in range(KVH * GROUP):
        part = q_ref[0, :, head * HD : (head + 1) * HD].astype(jnp.float32)
        g = head % GROUP
        qs[head // GROUP, :, g * HD : (g + 1) * HD] = turned(part, cosine, sine).astype(jnp.bfloat16)
    for head in range(KVH):
        part = k_ref[0, :, head * HD : (head + 1) * HD].astype(jnp.float32)
        ns[head, 0] = turned(part, cosine, sine).astype(jnp.bfloat16)
        ns[head, 1] = v_ref[0, :, head * HD : (head + 1) * HD]
    for i in (1, 2, 3):
        to = lax.rem(low + i, 4)
        send(qs.at[to], qa.at[low], c_send.at[0], c_recv.at[0], at_low(i))
        send(ns.at[to], na.at[ctx], c_send.at[1], c_recv.at[1], at_low(i))
    qa[low] = qs[low]
    na[ctx] = ns[low]

    back = jnp.zeros((8, HD), jnp.int32) - offset_ref[0]
    past_angles = (back.astype(jnp.float32) * freq)[0:1]
    past_cos, past_sin = jnp.cos(past_angles), jnp.sin(past_angles) * sign

    wait_for(hv.at[pl.ds(0, 3)], h_sem.at[1])
    to_smem = pltpu.make_async_copy(hv, hs, l_sem)
    to_smem.start()
    to_smem.wait()

    def name_of(r, p):
        return hs[plane(r), p, 0]

    def picked(r, h, p):
        return rx[r][h][name_of(r, p) & 15]

    def x_wait(r, h):
        wait_for(rx[r][h], x_recv.at[r, h])

    low_half, high_half = pl.ds(0, HALF), pl.ds(HALF, HALF)

    for h in range(NH):
        x_wait(2, h)
        for p in range(PPD):
            s2[h, p] = picked(2, h, p)
        send(s2.at[h, low_half], via_a.at[h], z_send.at[0, h], z_recv.at[0, h], at_plane(1))
        send(s2.at[h, high_half], via_b.at[h], z_send.at[1, h], z_recv.at[1, h], at_plane(3))

    def gather_new():
        wait_for(na.at[pl.ds(0, 3)], c_recv.at[1])
        wait_for(qa.at[pl.ds(0, 3)], c_recv.at[0])
        for i in (1, 2, 3):
            block = na.at[pl.ds(y * 4, 4)]
            send(block, block, c_send.at[2], c_recv.at[2], at_y(i))

    for h in range(NH):
        x_wait(1, h)
        for p in range(HALF, PPD):
            s1[h, p] = picked(1, h, p)
        send(s1.at[h, high_half], left.at[h, high_half], z_send.at[2, h], z_recv.at[2, h], at_plane(1))
        x_wait(3, h)
        for p in range(HALF):
            s3[h, p] = picked(3, h, p)
        send(s3.at[h, low_half], right.at[h, low_half], z_send.at[3, h], z_recv.at[3, h], at_plane(3))
        if h == 0:
            gather_new()
        wait_for(via_a.at[h], z_recv.at[0, h])
        for p in range(HALF):
            s1[h, p] = jnp.where((name_of(1, p) >> 4) == z, picked(1, h, p), via_a[h, p])
        send(s1.at[h, low_half], left.at[h, low_half], z_send.at[4, h], z_recv.at[4, h], at_plane(1))
        wait_for(via_b.at[h], z_recv.at[1, h])
        for p in range(HALF, PPD):
            s3[h, p] = jnp.where((name_of(3, p) >> 4) == z, picked(3, h, p), via_b[h, p - HALF])
        send(s3.at[h, high_half], right.at[h, high_half], z_send.at[5, h], z_recv.at[5, h], at_plane(3))

    for i in range(4):
        for g in range(GROUP):
            qm[i, g * 16 : (g + 1) * 16] = qa[i, :, g * HD : (g + 1) * HD]

    def scored(i, keys):
        return lax.dot_general(qm[i], keys, (((1,), (1,)), ((), ())), preferred_element_type=jnp.float32)

    wait_for(na.at[pl.ds(0, 12)], c_recv.at[2])
    new_keys = na[:, 0].reshape(256, HD)
    new_values = na[:, 1].reshape(256, HD)

    def start_rows(i, carry):
        token = (y * 4 + i) * 16 + (lax.broadcasted_iota(jnp.int32, (128, 256), 0) & 15)
        live = lax.broadcasted_iota(jnp.int32, (128, 256), 1) <= token
        scores = jnp.where(live, scored(i, new_keys), MASKED)
        highest = jnp.max(scores, axis=-1, keepdims=True)
        weights = jnp.exp2((scores - highest) * SCALE2)
        top[i] = jnp.broadcast_to(highest, (128, 128))
        tot[i] = jnp.broadcast_to(jnp.sum(weights, axis=-1, keepdims=True), (128, 128))
        acc[i] = jnp.dot(weights.astype(jnp.bfloat16), new_values, preferred_element_type=jnp.float32)
        return carry

    lax.fori_loop(0, 4, start_rows, 0)

    for h in range(NH):
        x_wait(0, h)
        for n in (2, 4):
            wait_for(left.at[h, low_half], z_recv.at[n, h])
        for n in (3, 5):
            wait_for(right.at[h, low_half], z_recv.at[n, h])
        wait_for(s2.at[h, low_half], z_send.at[0, h])
        wait_for(s2.at[h, high_half], z_send.at[1, h])
        for p in range(PPD):
            home = name_of(0, p) >> 4
            if p < HALF:
                far = jnp.where(home == plane(1), right[h, p], left[h, p])
            else:
                far = jnp.where(home == plane(3), left[h, p], right[h, p])
            page = jnp.where(home == z, picked(0, h, p), far)
            s2[h, p] = page
        pages = s2[h].reshape(ROWS, 2, KVH * HD)
        past_keys = pages[:, 0, :].astype(jnp.float32)
        past_values = pages[:, 1, :]
        for head in range(KVH):
            part = past_keys[:, head * HD : (head + 1) * HD]
            ks[h, head, 0] = turned(part, past_cos, past_sin).astype(jnp.bfloat16)
            ks[h, head, 1] = past_values[:, head * HD : (head + 1) * HD]
        for i in (1, 2, 3):
            to = lax.rem(low + i, 4)
            send(ks.at[h, to], ka.at[h, ctx], c_send.at[3 + h], c_recv.at[3 + h], at_low(i))
        ka[h, ctx] = ks[h, low]
        wait_for(ka.at[h, pl.ds(0, 3)], c_recv.at[3 + h])
        for i in (1, 2, 3):
            block = ka.at[h, pl.ds(y * 4, 4)]
            send(block, block, c_send.at[3 + NH + h], c_recv.at[3 + NH + h], at_y(i))
        wait_for(ka.at[h, pl.ds(0, 12)], c_recv.at[3 + NH + h])

        count = 16 * ROWS
        keys = ka[h, :, 0].reshape(count, HD)
        values = ka[h, :, 1].reshape(count, HD)
        at = lax.broadcasted_iota(jnp.int32, (1, count), 1)
        within = lax.rem(at, ROWS)
        index = (at // ROWS) * (PPD * PAGE) + (within // T) * PAGE + h * T + lax.rem(within, T)
        dead = jnp.where(index < length_ref[0], 0.0, MASKED)

        def add_rows(i, carry, keys=keys, values=values, dead=dead):
            scores = scored(i, keys) + dead
            before = top[i][:, 0:1]
            highest = jnp.maximum(before, jnp.max(scores, axis=-1, keepdims=True))
            weights = jnp.exp2((scores - highest) * SCALE2)
            shrink = jnp.exp2((before - highest) * SCALE2)
            top[i] = jnp.broadcast_to(highest, (128, 128))
            tot[i] = tot[i] * shrink + jnp.sum(weights, axis=-1, keepdims=True)
            acc[i] = acc[i] * shrink + jnp.dot(
                weights.astype(jnp.bfloat16), values, preferred_element_type=jnp.float32
            )
            return carry

        if h < NH - 1:
            lax.fori_loop(0, 4, add_rows, 0)
        else:
            for step in (1, 2, 3, 0):
                to = lax.rem(low + step, 4)
                add_rows(to, 0)
                result = (acc[to] / tot[to]).astype(jnp.bfloat16)
                for g in range(GROUP):
                    os_[to, :, g * HD : (g + 1) * HD] = result[g * 16 : (g + 1) * 16]
                if step:
                    send(os_.at[to], oa.at[low], c_send.at[3 + 2 * NH], c_recv.at[3 + 2 * NH], at_low(step))
                else:
                    oa[low] = os_[low]
    wait_for(oa.at[pl.ds(0, 3)], c_recv.at[3 + 2 * NH])
    for i in range(4):
        out_ref[0, :, i * GROUP * HD : (i + 1) * GROUP * HD] = oa[i]

    wait_for(hv.at[pl.ds(0, 3)], h_sem.at[0])
    for h in range(NH):
        for r in range(4):
            wait_for(rx[r][h].at[pl.ds(0, 14)], x_send.at[r, h])
        for n in (2, 3, 4, 5):
            wait_for(s1.at[h, low_half], z_send.at[n, h])
        wait_for(ks.at[h, pl.ds(0, 3)], c_send.at[3 + h])
        wait_for(ka.at[h, pl.ds(0, 12)], c_send.at[3 + NH + h])
    wait_for(qs.at[pl.ds(0, 3)], c_send.at[0])
    wait_for(ns.at[pl.ds(0, 3)], c_send.at[1])
    wait_for(na.at[pl.ds(0, 12)], c_send.at[2])
    wait_for(os_.at[pl.ds(0, 3)], c_send.at[3 + 2 * NH])


def body(page_store, page_holder, history_length, old_offset, turn_query, turn_key, turn_value):
    middle = np.arange(HD // 2, dtype=np.float32) * np.float32(2.0 / HD)
    freq = (ROPE_BASE ** -middle.astype(np.float64)).astype(np.float32)
    rows = np.zeros((8, HD), np.float32)
    rows[0] = np.concatenate([freq, freq])
    rows[1] = np.concatenate([-np.ones(HD // 2), np.ones(HD // 2)])
    bf16 = jnp.bfloat16
    part = (T, 2, KVH * HD)
    vmem = pltpu.VMEM
    scratch = [vmem((16,) + part, bf16) for _ in range(4 * NH)]
    scratch += [vmem((NH, PPD) + part, bf16) for _ in range(3)]
    scratch += [vmem((NH, HALF) + part, bf16) for _ in range(2)]
    scratch += [vmem((NH, PPD) + part, bf16) for _ in range(2)]
    scratch += [
        vmem((NH, 4, 2, ROWS, HD), bf16),
        vmem((NH, 16, 2, ROWS, HD), bf16),
        vmem((4, 2, 16, HD), bf16),
        vmem((16, 2, 16, HD), bf16),
        vmem((4, 16, GROUP * HD), bf16),
        vmem((4, 16, GROUP * HD), bf16),
        vmem((4, 128, HD), bf16),
        vmem((4, 16, GROUP * HD), bf16),
        vmem((4, 16, GROUP * HD), bf16),
        vmem((4, PPD, 128), jnp.int32),
        pltpu.SMEM((4, PPD, 128), jnp.int32),
        vmem((4, 128, HD), jnp.float32),
        vmem((4, 128, 128), jnp.float32),
        vmem((4, 128, 128), jnp.float32),
        pltpu.SemaphoreType.DMA((4, NH)),
        pltpu.SemaphoreType.DMA((4, NH)),
        pltpu.SemaphoreType.DMA((6, NH)),
        pltpu.SemaphoreType.DMA((6, NH)),
        pltpu.SemaphoreType.DMA((4 + 2 * NH,)),
        pltpu.SemaphoreType.DMA((4 + 2 * NH,)),
        pltpu.SemaphoreType.DMA((2,)),
        pltpu.SemaphoreType.DMA,
    ]
    in_smem = pl.BlockSpec(memory_space=pltpu.SMEM)
    in_vmem = pl.BlockSpec(memory_space=pltpu.VMEM)
    return pl.pallas_call(
        kernel,
        out_shape=jax.ShapeDtypeStruct(turn_query.shape, bf16),
        in_specs=[in_smem, in_smem, in_smem, in_vmem, pl.BlockSpec(memory_space=pl.ANY), in_vmem, in_vmem, in_vmem],
        out_specs=in_vmem,
        scratch_shapes=scratch,
        compiler_params=pltpu.CompilerParams(
            collective_id=0, has_side_effects=True, vmem_limit_bytes=48 * 1024 * 1024
        ),
        name="restore_attend",
    )(page_holder, history_length, old_offset, jnp.asarray(rows), page_store, turn_query, turn_key, turn_value)


def solution(mesh):
    placed = (
        P("sess", "ctx", None, None, None, None, None),
        P("sess", "ctx", None),
        P("sess"),
        P("sess"),
        P("sess", "ctx", None),
        P("sess", "ctx", None),
        P("sess", "ctx", None),
    )
    return jax.shard_map(
        body, mesh=mesh, in_specs=placed, out_specs=P("sess", "ctx", None), check_vma=False
    )
```

```python
import functools

import jax
import jax.numpy as jnp
import numpy as np
from jax import lax
from jax.experimental import pallas as pl
from jax.experimental.pallas import tpu as pltpu
from jax.sharding import PartitionSpec as P

MESH = pl.DeviceIdType.MESH
KVH = 4
GROUP = 8
HD = 128
PAGE = 16
PPD = 8
ROPE_BASE = 1000000.0
MASKED = -1e30
SCALE2 = HD ** (-0.5) * 1.4426950408889634
NX = 2
NZ = 4
TX = PAGE // NX
TZ = PAGE // NZ
PER = NZ // NX
ROWS = PPD * TZ
HALF = PPD // 2


def turned(v, cosine, sine):
    return v * cosine + pltpu.roll(v, HD // 2, 1) * sine


def wait_for(view, sem):
    pltpu.make_async_copy(view, view, sem).wait()


def kernel(hold_in, length_in, offset_in, freq_in, store, q_in, k_in, v_in, out_ref, *scratch):
    rx = [scratch[r * NX : (r + 1) * NX] for r in range(4)]
    (
        s0, s1, s2, s3, via_a, via_b, own, left, right, ka, ns, na, qs, qa, qm, os_, oa, hv, hs, mv, ms,
        acc, top, tot, hold_ref, length_ref, offset_ref, freq_ref, q_ref, k_ref, v_ref,
        x_send, x_recv, z_send, z_recv, y_send, y_recv, c_send, c_recv, h_sem, l_sem,
    ) = scratch[4 * NX :]
    fetched = [
        pltpu.make_async_copy(src, dst, l_sem.at[i])
        for i, (src, dst) in enumerate(
            [
                (hold_in, hold_ref), (length_in, length_ref), (offset_in, offset_ref), (freq_in, freq_ref),
                (q_in, q_ref), (k_in, k_ref), (v_in, v_ref),
            ]
        )
    ]
    for copy in fetched:
        copy.start()
    sess = lax.axis_index("sess")
    ctx = lax.axis_index("ctx")
    z, eighth = sess // 8, sess % 8
    x, core = eighth // 2, eighth % 2
    y, low = ctx // 4, ctx % 4

    def plane(step):
        return lax.rem(z + step, 4)

    def at_plane(step, low_step=0):
        return (plane(step) * 8 + eighth, y * 4 + lax.rem(low + low_step, 4))

    def mate(dx, dc):
        return lax.rem(x + dx, 4) * 2 + lax.rem(core + dc, 2)

    def at_low(step):
        return (sess, y * 4 + lax.rem(low + step, 4))

    def at_y(step):
        return (sess, lax.rem(y + step, 4) * 4 + low)

    mates = [(dx, dc) for dx in (2, 1, 3, 0) for dc in (0, 1) if (dx, dc) != (0, 0)]

    barrier = pltpu.get_barrier_semaphore()
    others = [at_plane(i, j) for j in (3, 2, 1, 0) for i in (1, 3)]
    others += [at_low(i) for i in (1, 2, 3)] + [at_y(i) for i in (1, 2, 3)]
    others += [(z * 8 + mate(*m), ctx) for m in mates]
    for other in others:
        pl.semaphore_signal(barrier, inc=1, device_id=other, device_id_type=MESH)

    fetched[0].wait()
    names = []
    for p in range(PPD):
        rank = jnp.int32(0)
        for e in range(p):
            rank = rank + jnp.where(hold_ref[0, e] == hold_ref[0, p], 1, 0).astype(jnp.int32)
        names.append(hold_ref[0, p] * 2 + rank)
    row = lax.broadcasted_iota(jnp.int32, (PPD, 128), 0)
    table = jnp.zeros((PPD, 128), jnp.int32)
    for p in range(PPD):
        table = jnp.where(row == p, names[p], table)
    hv[z] = table
    mv[low] = table

    pl.semaphore_wait(barrier, len(others))

    drain = []

    def send(src, dst, send_sem, recv_sem, to):
        pltpu.make_async_remote_copy(
            src_ref=src, dst_ref=dst, send_sem=send_sem, recv_sem=recv_sem, device_id=to, device_id_type=MESH
        ).start()

    for i in (1, 3):
        send(hv.at[z], hv.at[z], h_sem.at[0], h_sem.at[1], at_plane(i))
    for i in (1, 2, 3):
        send(mv.at[low], mv.at[low], h_sem.at[3], h_sem.at[4], at_low(i))
    drain += [(hv.at[pl.ds(0, 3)], h_sem.at[0]), (mv.at[pl.ds(0, 3)], h_sem.at[3])]

    order = [(0, 0)] + [(2, h) for h in range(NX)]
    for h in range(NX):
        order += ([(0, h)] if h else []) + [(1, h), (3, h)]
    for r, h in order:
        mine = pl.ds(eighth * 2, 2)
        tokens = pl.ds(h * TX, TX)
        for m in mates:
            other = mate(*m)
            send(
                store.at[0, 0, plane(r) * 8 + other, :, tokens], rx[r][h].at[mine],
                x_send.at[r, h], x_recv.at[r, h], (z * 8 + other, ctx),
            )
        pltpu.make_async_copy(
            store.at[0, 0, plane(r) * 8 + eighth, :, tokens], rx[r][h].at[mine], x_recv.at[r, h]
        ).start()
        drain.append((rx[r][h].at[pl.ds(0, 14)], x_send.at[r, h]))

    for copy in fetched[1:]:
        copy.wait()
    freq = freq_ref[0:1, :]
    sign = freq_ref[1:2, :]
    places = length_ref[0] + ctx * 16 + lax.broadcasted_iota(jnp.int32, (16, HD), 0)
    angles = places.astype(jnp.float32) * freq
    cosine, sine = jnp.cos(angles), jnp.sin(angles) * sign
    for head in range(KVH * GROUP):
        part = q_ref[0, :, head * HD : (head + 1) * HD].astype(jnp.float32)
        g = head % GROUP
        qs[head // GROUP, :, g * HD : (g + 1) * HD] = turned(part, cosine, sine).astype(jnp.bfloat16)
    for head in range(KVH):
        part = k_ref[0, :, head * HD : (head + 1) * HD].astype(jnp.float32)
        ns[head, 0] = turned(part, cosine, sine).astype(jnp.bfloat16)
        ns[head, 1] = v_ref[0, :, head * HD : (head + 1) * HD]
    for i in (1, 2, 3):
        to = lax.rem(low + i, 4)
        send(qs.at[to], qa.at[low], c_send.at[0], c_recv.at[0], at_low(i))
        send(ns.at[to], na.at[ctx], c_send.at[1], c_recv.at[1], at_low(i))
    drain += [(qs.at[pl.ds(0, 3)], c_send.at[0]), (ns.at[pl.ds(0, 3)], c_send.at[1])]
    qa[low] = qs[low]
    na[ctx] = ns[low]

    back = jnp.zeros((8, HD), jnp.int32) - offset_ref[0]
    past_angles = (back.astype(jnp.float32) * freq)[0:1]
    past_cos, past_sin = jnp.cos(past_angles), jnp.sin(past_angles) * sign

    wait_for(hv.at[pl.ds(0, 2)], h_sem.at[1])
    send(hv.at[plane(3)], hv.at[plane(3)], h_sem.at[0], h_sem.at[2], at_plane(1))
    wait_for(mv.at[pl.ds(0, 3)], h_sem.at[4])
    to_smem = pltpu.make_async_copy(mv, ms, l_sem.at[7])
    to_smem.start()
    to_smem.wait()

    def picked(r, h, p, name):
        part = h % PER
        return rx[r][h // PER][name & 15, part * TZ : (part + 1) * TZ]

    def x_wait(r, h):
        if h % PER == 0:
            wait_for(rx[r][h // PER], x_recv.at[r, h // PER])

    low_half, high_half = pl.ds(0, HALF), pl.ds(HALF, HALF)

    def by_head(ref, h, p, page):
        for head in range(KVH):
            ref[h, head, p] = page[:, :, head * HD : (head + 1) * HD]

    def pass_own(h):
        x_wait(0, h)
        for p in range(PPD):
            by_head(s0, h, p, picked(0, h, p, ms[low, p, 0]))
        for i in (1, 2, 3):
            to = lax.rem(low + i, 4)
            send(s0.at[h, to], own.at[h, low], z_send.at[0, h], z_recv.at[0, h], at_low(i))
        drain.append((s0.at[h, pl.ds(0, 3)], z_send.at[0, h]))
        own[h, low] = s0[h, low]

    for h in range(PER):
        pass_own(h)

    wait_for(hv.at[0], h_sem.at[2])
    to_smem = pltpu.make_async_copy(hv, hs, l_sem.at[7])
    to_smem.start()
    to_smem.wait()

    def name_of(r, p):
        return hs[plane(r), p, 0]

    for h in range(NZ):
        x_wait(2, h)
        for p in range(PPD):
            s2[h, p] = picked(2, h, p, name_of(2, p))
        send(s2.at[h, low_half], via_a.at[h], z_send.at[1, h], z_recv.at[1, h], at_plane(1))
        send(s2.at[h, high_half], via_b.at[h], z_send.at[2, h], z_recv.at[2, h], at_plane(3))
        drain += [(s2.at[h, low_half], z_send.at[1, h]), (s2.at[h, high_half], z_send.at[2, h])]

    def gather_new():
        wait_for(na.at[pl.ds(0, 3)], c_recv.at[1])
        wait_for(qa.at[pl.ds(0, 3)], c_recv.at[0])
        for i in (1, 2, 3):
            block = na.at[pl.ds(y * 4, 4)]
            send(block, block, c_send.at[2], c_recv.at[2], at_y(i))
        drain.append((na.at[pl.ds(0, 12)], c_send.at[2]))

    def spread(src, dst, h, half, n, step):
        for i in (0, 1, 2, 3):
            to = lax.rem(low + i, 4)
            send(src.at[h, to, half], dst.at[h, low, half], z_send.at[n, h], z_recv.at[n, h], at_plane(step, i))
        drain.append((src.at[h, pl.ds(0, 2)], z_send.at[n, h]))

    for h in range(NZ):
        if h >= PER:
            pass_own(h)
        x_wait(1, h)
        for p in range(HALF, PPD):
            by_head(s1, h, p, picked(1, h, p, name_of(1, p)))
        spread(s1, left, h, high_half, 3, 1)
        x_wait(3, h)
        for p in range(HALF):
            by_head(s3, h, p, picked(3, h, p, name_of(3, p)))
        spread(s3, right, h, low_half, 4, 3)
        if h == 0:
            gather_new()
        wait_for(via_a.at[h], z_recv.at[1, h])
        for p in range(HALF):
            name = name_of(1, p)
            by_head(s1, h, p, jnp.where((name >> 4) == z, picked(1, h, p, name), via_a[h, p]))
        spread(s1, left, h, low_half, 5, 1)
        wait_for(via_b.at[h], z_recv.at[2, h])
        for p in range(HALF, PPD):
            name = name_of(3, p)
            by_head(s3, h, p, jnp.where((name >> 4) == z, picked(3, h, p, name), via_b[h, p - HALF]))
        spread(s3, right, h, high_half, 6, 3)

    for i in range(4):
        for g in range(GROUP):
            qm[i, g * 16 : (g + 1) * 16] = qa[i, :, g * HD : (g + 1) * HD]

    def scored(i, keys):
        return lax.dot_general(qm[i], keys, (((1,), (1,)), ((), ())), preferred_element_type=jnp.float32)

    wait_for(na.at[pl.ds(0, 12)], c_recv.at[2])
    new_keys = na[:, 0].reshape(256, HD)
    new_values = na[:, 1].reshape(256, HD)

    def start_rows(i, carry):
        token = (y * 4 + i) * 16 + (lax.broadcasted_iota(jnp.int32, (128, 256), 0) & 15)
        live = lax.broadcasted_iota(jnp.int32, (128, 256), 1) <= token
        scores = jnp.where(live, scored(i, new_keys), MASKED)
        highest = jnp.max(scores, axis=-1, keepdims=True)
        weights = jnp.exp2((scores - highest) * SCALE2)
        top[i] = jnp.broadcast_to(highest, (128, 128))
        tot[i] = jnp.broadcast_to(jnp.sum(weights, axis=-1, keepdims=True), (128, 128))
        acc[i] = jnp.dot(weights.astype(jnp.bfloat16), new_values, preferred_element_type=jnp.float32)
        return carry

    lax.fori_loop(0, 4, start_rows, 0)

    def assemble(h):
        wait_for(own.at[h, pl.ds(0, 3)], z_recv.at[0, h])
        for n in (3, 5):
            wait_for(left.at[h, pl.ds(0, 2)], z_recv.at[n, h])
        for n in (4, 6):
            wait_for(right.at[h, pl.ds(0, 2)], z_recv.at[n, h])
        for i in range(4):
            pages = []
            for p in range(PPD):
                home = ms[i, p, 0] >> 4
                if p < HALF:
                    far = jnp.where(home == plane(1), right[h, i, p], left[h, i, p])
                else:
                    far = jnp.where(home == plane(3), left[h, i, p], right[h, i, p])
                pages.append(jnp.where(home == z, own[h, i, p], far))
            pages = jnp.concatenate(pages, axis=0)
            part = pages[:, 0, :].astype(jnp.float32)
            ka[h, y * 4 + i, 0] = turned(part, past_cos, past_sin).astype(jnp.bfloat16)
            ka[h, y * 4 + i, 1] = pages[:, 1, :]
        for i in (1, 2, 3):
            block = ka.at[h, pl.ds(y * 4, 4)]
            send(block, block, y_send.at[h], y_recv.at[h], at_y(i))
        drain.append((ka.at[h, pl.ds(0, 12)], y_send.at[h]))

    def attend(h, last):
        wait_for(ka.at[h, pl.ds(0, 12)], y_recv.at[h])
        count = 16 * ROWS
        keys = ka[h, :, 0].reshape(count, HD)
        values = ka[h, :, 1].reshape(count, HD)
        at = lax.broadcasted_iota(jnp.int32, (1, count), 1)
        within = lax.rem(at, ROWS)
        index = (at // ROWS) * (PPD * PAGE) + (within // TZ) * PAGE + h * TZ + lax.rem(within, TZ)
        dead = jnp.where(index < length_ref[0], 0.0, MASKED)

        def add_rows(i, carry):
            scores = scored(i, keys) + dead
            before = top[i][:, 0:1]
            highest = jnp.maximum(before, jnp.max(scores, axis=-1, keepdims=True))
            weights = jnp.exp2((scores - highest) * SCALE2)
            shrink = jnp.exp2((before - highest) * SCALE2)
            top[i] = jnp.broadcast_to(highest, (128, 128))
            tot[i] = tot[i] * shrink + jnp.sum(weights, axis=-1, keepdims=True)
            acc[i] = acc[i] * shrink + jnp.dot(
                weights.astype(jnp.bfloat16), values, preferred_element_type=jnp.float32
            )
            return carry

        if not last:
            lax.fori_loop(0, 4, add_rows, 0)
            return
        for step in (1, 2, 3, 0):
            to = lax.rem(low + step, 4)
            add_rows(to, 0)
            result = (acc[to] / tot[to]).astype(jnp.bfloat16)
            for g in range(GROUP):
                os_[to, :, g * HD : (g + 1) * HD] = result[g * 16 : (g + 1) * 16]
            if step:
                send(os_.at[to], oa.at[low], c_send.at[3], c_recv.at[3], at_low(step))
            else:
                oa[low] = os_[low]
        drain.append((os_.at[pl.ds(0, 3)], c_send.at[3]))

    for h in range(NZ):
        assemble(h)
        if h:
            attend(h - 1, False)
    attend(NZ - 1, True)
    wait_for(oa.at[pl.ds(0, 3)], c_recv.at[3])
    for i in range(4):
        out_ref[0, :, i * GROUP * HD : (i + 1) * GROUP * HD] = oa[i]

    for view, sem in drain:
        wait_for(view, sem)


def body(page_store, page_holder, history_length, old_offset, turn_query, turn_key, turn_value):
    middle = np.arange(HD // 2, dtype=np.float32) * np.float32(2.0 / HD)
    freq = (ROPE_BASE ** -middle.astype(np.float64)).astype(np.float32)
    rows = np.zeros((8, HD), np.float32)
    rows[0] = np.concatenate([freq, freq])
    rows[1] = np.concatenate([-np.ones(HD // 2), np.ones(HD // 2)])
    bf16 = jnp.bfloat16
    vmem = pltpu.VMEM
    page = (TZ, 2, KVH * HD)
    by_head = (NZ, KVH, PPD, TZ, 2, HD)
    scratch = [vmem((16, TX, 2, KVH * HD), bf16) for _ in range(4 * NX)]
    scratch += [
        vmem(by_head, bf16),
        vmem(by_head, bf16),
        vmem((NZ, PPD) + page, bf16),
        vmem(by_head, bf16),
        vmem((NZ, HALF) + page, bf16),
        vmem((NZ, HALF) + page, bf16),
        vmem(by_head, bf16),
        vmem(by_head, bf16),
        vmem(by_head, bf16),
        vmem((NZ, 16, 2, ROWS, HD), bf16),
        vmem((4, 2, 16, HD), bf16),
        vmem((16, 2, 16, HD), bf16),
        vmem((4, 16, GROUP * HD), bf16),
        vmem((4, 16, GROUP * HD), bf16),
        vmem((4, 128, HD), bf16),
        vmem((4, 16, GROUP * HD), bf16),
        vmem((4, 16, GROUP * HD), bf16),
        vmem((4, PPD, 128), jnp.int32),
        pltpu.SMEM((4, PPD, 128), jnp.int32),
        vmem((4, PPD, 128), jnp.int32),
        pltpu.SMEM((4, PPD, 128), jnp.int32),
        vmem((4, 128, HD), jnp.float32),
        vmem((4, 128, 128), jnp.float32),
        vmem((4, 128, 128), jnp.float32),
        pltpu.SMEM((1, PPD), jnp.int32),
        pltpu.SMEM((1,), jnp.int32),
        pltpu.SMEM((1,), jnp.int32),
        vmem((8, HD), jnp.float32),
        vmem(turn_query.shape, bf16),
        vmem(turn_key.shape, bf16),
        vmem(turn_value.shape, bf16),
        pltpu.SemaphoreType.DMA((4, NX)),
        pltpu.SemaphoreType.DMA((4, NX)),
        pltpu.SemaphoreType.DMA((7, NZ)),
        pltpu.SemaphoreType.DMA((7, NZ)),
        pltpu.SemaphoreType.DMA((NZ,)),
        pltpu.SemaphoreType.DMA((NZ,)),
        pltpu.SemaphoreType.DMA((4,)),
        pltpu.SemaphoreType.DMA((4,)),
        pltpu.SemaphoreType.DMA((5,)),
        pltpu.SemaphoreType.DMA((8,)),
    ]
    there = pl.BlockSpec(memory_space=pltpu.HBM)
    return pl.pallas_call(
        kernel,
        out_shape=jax.ShapeDtypeStruct(turn_query.shape, bf16),
        in_specs=[there] * 8,
        out_specs=pl.BlockSpec(memory_space=pltpu.VMEM),
        scratch_shapes=scratch,
        compiler_params=pltpu.CompilerParams(
            collective_id=0, has_side_effects=True, vmem_limit_bytes=64 * 1024 * 1024 - 65536
        ),
        name="restore_attend",
    )(page_holder.reshape(1, PPD), history_length, old_offset, jnp.asarray(rows), page_store, turn_query, turn_key, turn_value)


def solution(mesh):
    placed = (
        P("sess", "ctx", None, None, None, None, None),
        P("sess", "ctx", None),
        P("sess"),
        P("sess"),
        P("sess", "ctx", None),
        P("sess", "ctx", None),
        P("sess", "ctx", None),
    )
    return jax.shard_map(
        body, mesh=mesh, in_specs=placed, out_specs=P("sess", "ctx", None), check_vma=False
    )
```

```python
import functools

import jax
import jax.numpy as jnp
import numpy as np
from jax import lax
from jax.experimental import pallas as pl
from jax.experimental.pallas import tpu as pltpu
from jax.sharding import PartitionSpec as P

MESH = pl.DeviceIdType.MESH
KVH = 4
GROUP = 8
HD = 128
PAGE = 16
PPD = 8
ROPE_BASE = 1000000.0
MASKED = -1e30
SCALE2 = HD ** (-0.5) * 1.4426950408889634
PARTS = ((0, 2), (2, 4), (6, 4), (10, 4), (14, 2))
NZ = len(PARTS)
HALF = PPD // 2
ORDER = ((0, 0), (1, 0), (3, 0), (1, 1), (3, 1), (2, 0), (2, 1), (2, 2), (2, 3), (2, 4), (0, 1))
ORDER += tuple((r, h) for h in range(2, NZ) for r in (0, 1, 3))


def turned(v, cosine, sine):
    return v * cosine + pltpu.roll(v, HD // 2, 1) * sine


def wait_for(view, sem):
    pltpu.make_async_copy(view, view, sem).wait()


def kernel(hold_in, length_in, offset_in, freq_in, store, q_in, k_in, v_in, out_ref, *scratch):
    rx = [scratch[r * NZ : (r + 1) * NZ] for r in range(4)]
    lists = scratch[4 * NZ :]
    s0, s1, s2, s3, via_a, via_b, own, left, right, ka = (lists[i * NZ : (i + 1) * NZ] for i in range(10))
    (
        ns, na, qs, qa, qm, os_, oa, hv, hs, mv, ms,
        acc, top, tot, hold_ref, length_ref, offset_ref, freq_ref, q_ref, k_ref, v_ref,
        x_send, x_recv, z_send, z_recv, y_send, y_recv, c_send, c_recv, h_sem, l_sem,
    ) = lists[10 * NZ :]
    fetched = [
        pltpu.make_async_copy(src, dst, l_sem.at[i])
        for i, (src, dst) in enumerate(
            [
                (hold_in, hold_ref), (length_in, length_ref), (offset_in, offset_ref), (freq_in, freq_ref),
                (q_in, q_ref), (k_in, k_ref), (v_in, v_ref),
            ]
        )
    ]
    for copy in fetched:
        copy.start()
    sess = lax.axis_index("sess")
    ctx = lax.axis_index("ctx")
    z, eighth = sess // 8, sess % 8
    x, core = eighth // 2, eighth % 2
    y, low = ctx // 4, ctx % 4

    def plane(step):
        return lax.rem(z + step, 4)

    def at_plane(step, low_step=0):
        return (plane(step) * 8 + eighth, y * 4 + lax.rem(low + low_step, 4))

    def mate(dx, dc):
        return lax.rem(x + dx, 4) * 2 + lax.rem(core + dc, 2)

    def at_low(step):
        return (sess, y * 4 + lax.rem(low + step, 4))

    def at_y(step):
        return (sess, lax.rem(y + step, 4) * 4 + low)

    mates = [(dx, dc) for dx in (2, 1, 3, 0) for dc in (0, 1) if (dx, dc) != (0, 0)]

    barrier = pltpu.get_barrier_semaphore()
    others = [at_plane(i, j) for j in (3, 2, 1, 0) for i in (1, 3)]
    others += [at_low(i) for i in (1, 2, 3)] + [at_y(i) for i in (1, 2, 3)]
    others += [(z * 8 + mate(*m), ctx) for m in mates]
    for other in others:
        pl.semaphore_signal(barrier, inc=1, device_id=other, device_id_type=MESH)

    fetched[0].wait()
    names = []
    for p in range(PPD):
        rank = jnp.int32(0)
        for e in range(p):
            rank = rank + jnp.where(hold_ref[0, e] == hold_ref[0, p], 1, 0).astype(jnp.int32)
        names.append(hold_ref[0, p] * 2 + rank)
    row = lax.broadcasted_iota(jnp.int32, (PPD, 128), 0)
    table = jnp.zeros((PPD, 128), jnp.int32)
    for p in range(PPD):
        table = jnp.where(row == p, names[p], table)
    hv[z] = table
    mv[low] = table

    for copy in fetched[1:]:
        copy.wait()
    freq = freq_ref[0:1, :]
    sign = freq_ref[1:2, :]
    places = length_ref[0] + ctx * 16 + lax.broadcasted_iota(jnp.int32, (16, HD), 0)
    angles = places.astype(jnp.float32) * freq
    cosine, sine = jnp.cos(angles), jnp.sin(angles) * sign
    for head in range(KVH * GROUP):
        part = q_ref[0, :, head * HD : (head + 1) * HD].astype(jnp.float32)
        g = head % GROUP
        qs[head // GROUP, :, g * HD : (g + 1) * HD] = turned(part, cosine, sine).astype(jnp.bfloat16)
    for head in range(KVH):
        part = k_ref[0, :, head * HD : (head + 1) * HD].astype(jnp.float32)
        ns[head, 0] = turned(part, cosine, sine).astype(jnp.bfloat16)
        ns[head, 1] = v_ref[0, :, head * HD : (head + 1) * HD]
    back = jnp.zeros((8, HD), jnp.int32) - offset_ref[0]
    past_angles = (back.astype(jnp.float32) * freq)[0:1]
    past_cos, past_sin = jnp.cos(past_angles), jnp.sin(past_angles) * sign

    pl.semaphore_wait(barrier, len(others))

    drain = []

    def send(src, dst, send_sem, recv_sem, to):
        pltpu.make_async_remote_copy(
            src_ref=src, dst_ref=dst, send_sem=send_sem, recv_sem=recv_sem, device_id=to, device_id_type=MESH
        ).start()

    for i in (1, 3):
        send(hv.at[z], hv.at[z], h_sem.at[0], h_sem.at[1], at_plane(i))
    for i in (1, 2, 3):
        send(mv.at[low], mv.at[low], h_sem.at[3], h_sem.at[4], at_low(i))
    drain += [(hv.at[pl.ds(0, 3)], h_sem.at[0]), (mv.at[pl.ds(0, 3)], h_sem.at[3])]

    def send_queries():
        for i in (1, 2, 3):
            to = lax.rem(low + i, 4)
            send(qs.at[to], qa.at[low], c_send.at[0], c_recv.at[0], at_low(i))
            send(ns.at[to], na.at[ctx], c_send.at[1], c_recv.at[1], at_low(i))
        drain.extend([(qs.at[pl.ds(0, 3)], c_send.at[0]), (ns.at[pl.ds(0, 3)], c_send.at[1])])
        qa[low] = qs[low]
        na[ctx] = ns[low]

    for n, (r, h) in enumerate(ORDER):
        if n == 3:
            send_queries()
        mine = pl.ds(eighth * 2, 2)
        tokens = pl.ds(*PARTS[h])
        for m in mates:
            other = mate(*m)
            send(
                store.at[0, 0, plane(r) * 8 + other, :, tokens], rx[r][h].at[mine],
                x_send.at[r, h], x_recv.at[r, h], (z * 8 + other, ctx),
            )
        pltpu.make_async_copy(
            store.at[0, 0, plane(r) * 8 + eighth, :, tokens], rx[r][h].at[mine], x_recv.at[r, h]
        ).start()
        drain.append((rx[r][h].at[pl.ds(0, 14)], x_send.at[r, h]))

    def to_smem(src, dst, *rows):
        copies = [pltpu.make_async_copy(src.at[i], dst.at[i], l_sem.at[7 + n]) for n, i in enumerate(rows)]
        for copy in copies:
            copy.start()
        for copy in copies:
            copy.wait()

    def name_of(r, p):
        return hs[plane(r), p, 0]

    def picked(r, h, p, name):
        return rx[r][h][name & 15]

    def x_wait(r, h):
        wait_for(rx[r][h], x_recv.at[r, h])

    low_half, high_half = pl.ds(0, HALF), pl.ds(HALF, HALF)

    def by_head(ref, p, page):
        for head in range(KVH):
            ref[head, p] = page[:, :, head * HD : (head + 1) * HD]

    def pass_own(h):
        x_wait(0, h)
        for p in range(PPD):
            by_head(s0[h], p, picked(0, h, p, names[p]))
        for i in (1, 2, 3):
            to = lax.rem(low + i, 4)
            send(s0[h].at[to], own[h].at[low], z_send.at[0, h], z_recv.at[0, h], at_low(i))
        drain.append((s0[h].at[pl.ds(0, 3)], z_send.at[0, h]))
        own[h][low] = s0[h][low]

    def spread(src, dst, h, half, n, step):
        for to in (3, 2, 1, 0) if step == 1 else (0, 1, 2, 3):
            end = (plane(step) * 8 + eighth, y * 4 + to)
            send(src[h].at[to, half], dst[h].at[low, half], z_send.at[n, h], z_recv.at[n, h], end)
        drain.append((src[h].at[pl.ds(0, 2)], z_send.at[n, h]))

    def pass_direct(h):
        x_wait(1, h)
        for p in range(HALF, PPD):
            by_head(s1[h], p, picked(1, h, p, name_of(1, p)))
        spread(s1, left, h, high_half, 3, 1)
        x_wait(3, h)
        for p in range(HALF):
            by_head(s3[h], p, picked(3, h, p, name_of(3, p)))
        spread(s3, right, h, low_half, 4, 3)

    def pass_far(h):
        x_wait(2, h)
        for p in range(PPD):
            s2[h][p] = picked(2, h, p, name_of(2, p))
        send(s2[h].at[low_half], via_a[h], z_send.at[1, h], z_recv.at[1, h], at_plane(1))
        send(s2[h].at[high_half], via_b[h], z_send.at[2, h], z_recv.at[2, h], at_plane(3))
        drain.append((s2[h].at[low_half], z_send.at[1, h]))
        drain.append((s2[h].at[high_half], z_send.at[2, h]))

    def pass_merged(h):
        wait_for(via_a[h], z_recv.at[1, h])
        for p in range(HALF):
            name = name_of(1, p)
            by_head(s1[h], p, jnp.where((name >> 4) == z, picked(1, h, p, name), via_a[h][p]))
        spread(s1, left, h, low_half, 5, 1)
        wait_for(via_b[h], z_recv.at[2, h])
        for p in range(HALF, PPD):
            name = name_of(3, p)
            by_head(s3[h], p, jnp.where((name >> 4) == z, picked(3, h, p, name), via_b[h][p - HALF]))
        spread(s3, right, h, high_half, 6, 3)

    pass_own(0)
    wait_for(hv.at[pl.ds(0, 2)], h_sem.at[1])
    send(hv.at[plane(3)], hv.at[plane(3)], h_sem.at[0], h_sem.at[2], at_plane(1))
    to_smem(hv, hs, plane(1), plane(3))
    pass_direct(0)
    pass_direct(1)
    wait_for(hv.at[0], h_sem.at[2])
    to_smem(hv, hs, plane(2))
    for h in range(NZ):
        pass_far(h)
    wait_for(na.at[pl.ds(0, 3)], c_recv.at[1])
    wait_for(qa.at[pl.ds(0, 3)], c_recv.at[0])
    for i in (1, 2, 3):
        block = na.at[pl.ds(y * 4, 4)]
        send(block, block, c_send.at[2], c_recv.at[2], at_y(i))
    drain.append((na.at[pl.ds(0, 12)], c_send.at[2]))
    pass_merged(0)
    pass_own(1)
    pass_merged(1)
    for h in range(2, NZ):
        pass_own(h)
        pass_direct(h)
        pass_merged(h)

    wait_for(mv.at[pl.ds(0, 3)], h_sem.at[4])
    to_smem(mv, ms, 0, 1, 2, 3)

    for i in range(4):
        for g in range(GROUP):
            qm[i, g * 16 : (g + 1) * 16] = qa[i, :, g * HD : (g + 1) * HD]

    def scored(i, keys):
        return lax.dot_general(qm[i], keys, (((1,), (1,)), ((), ())), preferred_element_type=jnp.float32)

    wait_for(na.at[pl.ds(0, 12)], c_recv.at[2])
    new_keys = na[:, 0].reshape(256, HD)
    new_values = na[:, 1].reshape(256, HD)

    def start_rows(i, carry):
        token = (y * 4 + i) * 16 + (lax.broadcasted_iota(jnp.int32, (128, 256), 0) & 15)
        live = lax.broadcasted_iota(jnp.int32, (128, 256), 1) <= token
        scores = jnp.where(live, scored(i, new_keys), MASKED)
        highest = jnp.max(scores, axis=-1, keepdims=True)
        weights = jnp.exp2((scores - highest) * SCALE2)
        top[i] = jnp.broadcast_to(highest, (128, 128))
        tot[i] = jnp.broadcast_to(jnp.sum(weights, axis=-1, keepdims=True), (128, 128))
        acc[i] = jnp.dot(weights.astype(jnp.bfloat16), new_values, preferred_element_type=jnp.float32)
        return carry

    lax.fori_loop(0, 4, start_rows, 0)

    def assemble(h):
        wait_for(own[h].at[pl.ds(0, 3)], z_recv.at[0, h])
        for n in (3, 5):
            wait_for(left[h].at[pl.ds(0, 2)], z_recv.at[n, h])
        for n in (4, 6):
            wait_for(right[h].at[pl.ds(0, 2)], z_recv.at[n, h])
        for i in range(4):
            pages = []
            for p in range(PPD):
                home = ms[i, p, 0] >> 4
                if p < HALF:
                    far = jnp.where(home == plane(1), right[h][i, p], left[h][i, p])
                else:
                    far = jnp.where(home == plane(3), left[h][i, p], right[h][i, p])
                pages.append(jnp.where(home == z, own[h][i, p], far))
            pages = jnp.concatenate(pages, axis=0)
            part = pages[:, 0, :].astype(jnp.float32)
            ka[h][y * 4 + i, 0] = turned(part, past_cos, past_sin).astype(jnp.bfloat16)
            ka[h][y * 4 + i, 1] = pages[:, 1, :]
        for i in (1, 2, 3):
            block = ka[h].at[pl.ds(y * 4, 4)]
            send(block, block, y_send.at[h], y_recv.at[h], at_y(i))
        drain.append((ka[h].at[pl.ds(0, 12)], y_send.at[h]))

    def attend(h, last):
        wait_for(ka[h].at[pl.ds(0, 12)], y_recv.at[h])
        first, tokens = PARTS[h]
        rows = PPD * tokens
        count = 16 * rows
        keys = ka[h][:, 0].reshape(count, HD)
        values = ka[h][:, 1].reshape(count, HD)
        at = lax.broadcasted_iota(jnp.int32, (1, count), 1)
        within = lax.rem(at, rows)
        index = lax.div(at, rows) * (PPD * PAGE) + lax.div(within, tokens) * PAGE + first + lax.rem(within, tokens)
        dead = jnp.where(index < length_ref[0], 0.0, MASKED)

        def add_rows(i, carry):
            scores = scored(i, keys) + dead
            before = top[i][:, 0:1]
            highest = jnp.maximum(before, jnp.max(scores, axis=-1, keepdims=True))
            weights = jnp.exp2((scores - highest) * SCALE2)
            shrink = jnp.exp2((before - highest) * SCALE2)
            top[i] = jnp.broadcast_to(highest, (128, 128))
            tot[i] = tot[i] * shrink + jnp.sum(weights, axis=-1, keepdims=True)
            acc[i] = acc[i] * shrink + jnp.dot(
                weights.astype(jnp.bfloat16), values, preferred_element_type=jnp.float32
            )
            return carry

        if not last:
            lax.fori_loop(0, 4, add_rows, 0)
            return
        for step in (1, 2, 3, 0):
            to = lax.rem(low + step, 4)
            add_rows(to, 0)
            result = (acc[to] / tot[to]).astype(jnp.bfloat16)
            for g in range(GROUP):
                os_[to, :, g * HD : (g + 1) * HD] = result[g * 16 : (g + 1) * 16]
            if step:
                send(os_.at[to], oa.at[low], c_send.at[3], c_recv.at[3], at_low(step))
            else:
                oa[low] = os_[low]
        drain.append((os_.at[pl.ds(0, 3)], c_send.at[3]))

    for h in range(NZ):
        assemble(h)
        if h:
            attend(h - 1, False)
    attend(NZ - 1, True)
    wait_for(oa.at[pl.ds(0, 3)], c_recv.at[3])
    for i in range(4):
        out_ref[0, :, i * GROUP * HD : (i + 1) * GROUP * HD] = oa[i]

    for view, sem in drain:
        wait_for(view, sem)


def body(page_store, page_holder, history_length, old_offset, turn_query, turn_key, turn_value):
    middle = np.arange(HD // 2, dtype=np.float32) * np.float32(2.0 / HD)
    freq = (ROPE_BASE ** -middle.astype(np.float64)).astype(np.float32)
    rows = np.zeros((8, HD), np.float32)
    rows[0] = np.concatenate([freq, freq])
    rows[1] = np.concatenate([-np.ones(HD // 2), np.ones(HD // 2)])
    bf16 = jnp.bfloat16
    vmem = pltpu.VMEM
    wide = KVH * HD
    scratch = [vmem((16, tokens, 2, wide), bf16) for _ in range(4) for _, tokens in PARTS]

    def by_part(*shape):
        return [vmem(tuple(n or tokens for n in shape), bf16) for _, tokens in PARTS]

    scratch += by_part(KVH, PPD, 0, 2, HD) * 2 + by_part(PPD, 0, 2, wide) + by_part(KVH, PPD, 0, 2, HD)
    scratch += by_part(HALF, 0, 2, wide) * 2 + by_part(4, PPD, 0, 2, HD) * 3
    scratch += [vmem((16, 2, PPD * tokens, HD), bf16) for _, tokens in PARTS]
    scratch += [
        vmem((4, 2, 16, HD), bf16),
        vmem((16, 2, 16, HD), bf16),
        vmem((4, 16, GROUP * HD), bf16),
        vmem((4, 16, GROUP * HD), bf16),
        vmem((4, 128, HD), bf16),
        vmem((4, 16, GROUP * HD), bf16),
        vmem((4, 16, GROUP * HD), bf16),
        vmem((4, PPD, 128), jnp.int32),
        pltpu.SMEM((4, PPD, 128), jnp.int32),
        vmem((4, PPD, 128), jnp.int32),
        pltpu.SMEM((4, PPD, 128), jnp.int32),
        vmem((4, 128, HD), jnp.float32),
        vmem((4, 128, 128), jnp.float32),
        vmem((4, 128, 128), jnp.float32),
        pltpu.SMEM((1, PPD), jnp.int32),
        pltpu.SMEM((1,), jnp.int32),
        pltpu.SMEM((1,), jnp.int32),
        vmem((8, HD), jnp.float32),
        vmem(turn_query.shape, bf16),
        vmem(turn_key.shape, bf16),
        vmem(turn_value.shape, bf16),
        pltpu.SemaphoreType.DMA((4, NZ)),
        pltpu.SemaphoreType.DMA((4, NZ)),
        pltpu.SemaphoreType.DMA((7, NZ)),
        pltpu.SemaphoreType.DMA((7, NZ)),
        pltpu.SemaphoreType.DMA((NZ,)),
        pltpu.SemaphoreType.DMA((NZ,)),
        pltpu.SemaphoreType.DMA((4,)),
        pltpu.SemaphoreType.DMA((4,)),
        pltpu.SemaphoreType.DMA((5,)),
        pltpu.SemaphoreType.DMA((11,)),
    ]
    there = pl.BlockSpec(memory_space=pltpu.HBM)
    return pl.pallas_call(
        kernel,
        out_shape=jax.ShapeDtypeStruct(turn_query.shape, bf16),
        in_specs=[there] * 8,
        out_specs=pl.BlockSpec(memory_space=pltpu.VMEM),
        scratch_shapes=scratch,
        compiler_params=pltpu.CompilerParams(
            collective_id=0, has_side_effects=True, vmem_limit_bytes=64 * 1024 * 1024 - 65536
        ),
        name="restore_attend",
    )(page_holder.reshape(1, PPD), history_length, old_offset, jnp.asarray(rows), page_store, turn_query, turn_key, turn_value)


def solution(mesh):
    placed = (
        P("sess", "ctx", None, None, None, None, None),
        P("sess", "ctx", None),
        P("sess"),
        P("sess"),
        P("sess", "ctx", None),
        P("sess", "ctx", None),
        P("sess", "ctx", None),
    )
    return jax.shard_map(
        body, mesh=mesh, in_specs=placed, out_specs=P("sess", "ctx", None), check_vma=False
    )
```

```python
import functools

import jax
import jax.numpy as jnp
import numpy as np
from jax import lax
from jax.experimental import pallas as pl
from jax.experimental.pallas import tpu as pltpu
from jax.sharding import PartitionSpec as P

MESH = pl.DeviceIdType.MESH
KVH = 4
GROUP = 8
HD = 128
PAGE = 16
PPD = 8
ROPE_BASE = 1000000.0
MASKED = -1e30
SCALE2 = HD ** (-0.5) * 1.4426950408889634
PARTS = ((0, 2), (2, 4), (6, 4), (10, 4), (14, 2))
NZ = len(PARTS)
HALF = PPD // 2
ORDER = ((0, 0), (0, 1), (1, 0), (3, 0), (0, 2), (2, 0), (2, 1), (2, 2), (2, 3), (2, 4))
ORDER += ((0, 3), (1, 1), (3, 1), (1, 2), (3, 2), (1, 3), (3, 3), (0, 4), (1, 4), (3, 4))
PLAN = ("o0", "o1", "near", "d0", "o2", "far", "f0", "f1", "f2", "f3", "f4")
PLAN += ("o3", "new", "m0", "d1", "m1", "d2", "m2", "d3", "m3", "o4", "d4", "m4")


def turned(v, cosine, sine):
    return v * cosine + pltpu.roll(v, HD // 2, 1) * sine


def wait_for(view, sem):
    pltpu.make_async_copy(view, view, sem).wait()


def kernel(hold_in, length_in, offset_in, freq_in, store, q_in, k_in, v_in, out_ref, *scratch):
    rx = [scratch[r * NZ : (r + 1) * NZ] for r in range(4)]
    lists = scratch[4 * NZ :]
    s0, s1, s2, s3, via_a, via_b, own, left, right, ka = (lists[i * NZ : (i + 1) * NZ] for i in range(10))
    (
        ns, na, qs, qa, qm, os_, oa, hv, hs, mv, ms,
        acc, top, tot, hold_ref, length_ref, offset_ref, freq_ref, q_ref, k_ref, v_ref,
        x_send, x_recv, z_send, z_recv, y_send, y_recv, c_send, c_recv, h_sem, l_sem,
    ) = lists[10 * NZ :]
    fetched = [
        pltpu.make_async_copy(src, dst, l_sem.at[i])
        for i, (src, dst) in enumerate(
            [
                (hold_in, hold_ref), (length_in, length_ref), (offset_in, offset_ref), (freq_in, freq_ref),
                (q_in, q_ref), (k_in, k_ref), (v_in, v_ref),
            ]
        )
    ]
    for copy in fetched:
        copy.start()
    sess = lax.axis_index("sess")
    ctx = lax.axis_index("ctx")
    z, eighth = sess // 8, sess % 8
    x, core = eighth // 2, eighth % 2
    y, low = ctx // 4, ctx % 4

    def plane(step):
        return lax.rem(z + step, 4)

    def at_plane(step, low_step=0):
        return (plane(step) * 8 + eighth, y * 4 + lax.rem(low + low_step, 4))

    def mate(dx, dc):
        return lax.rem(x + dx, 4) * 2 + lax.rem(core + dc, 2)

    def at_low(step):
        return (sess, y * 4 + lax.rem(low + step, 4))

    def at_y(step):
        return (sess, lax.rem(y + step, 4) * 4 + low)

    mates = [(dx, dc) for dx in (2, 1, 3, 0) for dc in (0, 1) if (dx, dc) != (0, 0)]

    barrier = pltpu.get_barrier_semaphore()
    others = [at_plane(i, j) for j in (3, 2, 1, 0) for i in (1, 3)]
    others += [at_low(i) for i in (1, 2, 3)] + [at_y(i) for i in (1, 2, 3)]
    others += [(z * 8 + mate(*m), ctx) for m in mates]
    for other in others:
        pl.semaphore_signal(barrier, inc=1, device_id=other, device_id_type=MESH)

    fetched[0].wait()
    names = []
    for p in range(PPD):
        rank = jnp.int32(0)
        for e in range(p):
            rank = rank + jnp.where(hold_ref[0, e] == hold_ref[0, p], 1, 0).astype(jnp.int32)
        names.append(hold_ref[0, p] * 2 + rank)
    row = lax.broadcasted_iota(jnp.int32, (PPD, 128), 0)
    table = jnp.zeros((PPD, 128), jnp.int32)
    for p in range(PPD):
        table = jnp.where(row == p, names[p], table)
    hv[z] = table
    mv[low] = table

    for copy in fetched[1:]:
        copy.wait()
    freq = freq_ref[0:1, :]
    sign = freq_ref[1:2, :]
    places = length_ref[0] + ctx * 16 + lax.broadcasted_iota(jnp.int32, (16, HD), 0)
    angles = places.astype(jnp.float32) * freq
    cosine, sine = jnp.cos(angles), jnp.sin(angles) * sign
    for head in range(KVH * GROUP):
        part = q_ref[0, :, head * HD : (head + 1) * HD].astype(jnp.float32)
        g = head % GROUP
        qs[head // GROUP, :, g * HD : (g + 1) * HD] = turned(part, cosine, sine).astype(jnp.bfloat16)
    for head in range(KVH):
        part = k_ref[0, :, head * HD : (head + 1) * HD].astype(jnp.float32)
        ns[head, 0] = turned(part, cosine, sine).astype(jnp.bfloat16)
        ns[head, 1] = v_ref[0, :, head * HD : (head + 1) * HD]
    back = jnp.zeros((8, HD), jnp.int32) - offset_ref[0]
    past_angles = (back.astype(jnp.float32) * freq)[0:1]
    past_cos, past_sin = jnp.cos(past_angles), jnp.sin(past_angles) * sign

    pl.semaphore_wait(barrier, len(others))

    drain = []

    def send(src, dst, send_sem, recv_sem, to):
        pltpu.make_async_remote_copy(
            src_ref=src, dst_ref=dst, send_sem=send_sem, recv_sem=recv_sem, device_id=to, device_id_type=MESH
        ).start()

    for i in (1, 3):
        send(hv.at[z], hv.at[z], h_sem.at[0], h_sem.at[1], at_plane(i))
    for i in (1, 2, 3):
        send(mv.at[low], mv.at[low], h_sem.at[3], h_sem.at[4], at_low(i))
    drain += [(hv.at[pl.ds(0, 3)], h_sem.at[0]), (mv.at[pl.ds(0, 3)], h_sem.at[3])]

    def send_queries():
        for i in (1, 2, 3):
            to = lax.rem(low + i, 4)
            send(qs.at[to], qa.at[low], c_send.at[0], c_recv.at[0], at_low(i))
            send(ns.at[to], na.at[ctx], c_send.at[1], c_recv.at[1], at_low(i))
        drain.extend([(qs.at[pl.ds(0, 3)], c_send.at[0]), (ns.at[pl.ds(0, 3)], c_send.at[1])])
        qa[low] = qs[low]
        na[ctx] = ns[low]

    for n, (r, h) in enumerate(ORDER):
        if n == 3:
            send_queries()
        mine = pl.ds(eighth * 2, 2)
        tokens = pl.ds(*PARTS[h])
        for m in mates:
            other = mate(*m)
            send(
                store.at[0, 0, plane(r) * 8 + other, :, tokens], rx[r][h].at[mine],
                x_send.at[r, h], x_recv.at[r, h], (z * 8 + other, ctx),
            )
        pltpu.make_async_copy(
            store.at[0, 0, plane(r) * 8 + eighth, :, tokens], rx[r][h].at[mine], x_recv.at[r, h]
        ).start()
        drain.append((rx[r][h].at[pl.ds(0, 14)], x_send.at[r, h]))

    def to_smem(src, dst, *rows):
        copies = [pltpu.make_async_copy(src.at[i], dst.at[i], l_sem.at[7 + n]) for n, i in enumerate(rows)]
        for copy in copies:
            copy.start()
        for copy in copies:
            copy.wait()

    def name_of(r, p):
        return hs[plane(r), p, 0]

    def picked(r, h, p, name):
        return rx[r][h][name & 15]

    def x_wait(r, h):
        wait_for(rx[r][h], x_recv.at[r, h])

    low_half, high_half = pl.ds(0, HALF), pl.ds(HALF, HALF)

    def by_head(ref, p, page):
        for head in range(KVH):
            ref[head, p] = page[:, :, head * HD : (head + 1) * HD]

    def pass_own(h):
        x_wait(0, h)
        for p in range(PPD):
            by_head(s0[h], p, picked(0, h, p, names[p]))
        for i in (1, 2, 3):
            to = lax.rem(low + i, 4)
            send(s0[h].at[to], own[h].at[low], z_send.at[0, h], z_recv.at[0, h], at_low(i))
        drain.append((s0[h].at[pl.ds(0, 3)], z_send.at[0, h]))
        own[h][low] = s0[h][low]

    def spread(src, dst, h, half, n, step):
        for to in (3, 2, 1, 0) if step == 1 else (0, 1, 2, 3):
            end = (plane(step) * 8 + eighth, y * 4 + to)
            send(src[h].at[to, half], dst[h].at[low, half], z_send.at[n, h], z_recv.at[n, h], end)
        drain.append((src[h].at[pl.ds(0, 2)], z_send.at[n, h]))

    def pass_direct(h):
        x_wait(1, h)
        for p in range(HALF, PPD):
            by_head(s1[h], p, picked(1, h, p, name_of(1, p)))
        spread(s1, left, h, high_half, 3, 1)
        x_wait(3, h)
        for p in range(HALF):
            by_head(s3[h], p, picked(3, h, p, name_of(3, p)))
        spread(s3, right, h, low_half, 4, 3)

    def pass_far(h):
        x_wait(2, h)
        for p in range(PPD):
            s2[h][p] = picked(2, h, p, name_of(2, p))
        send(s2[h].at[low_half], via_a[h], z_send.at[1, h], z_recv.at[1, h], at_plane(1))
        send(s2[h].at[high_half], via_b[h], z_send.at[2, h], z_recv.at[2, h], at_plane(3))
        drain.append((s2[h].at[low_half], z_send.at[1, h]))
        drain.append((s2[h].at[high_half], z_send.at[2, h]))

    def pass_merged(h):
        wait_for(via_a[h], z_recv.at[1, h])
        for p in range(HALF):
            name = name_of(1, p)
            by_head(s1[h], p, jnp.where((name >> 4) == z, picked(1, h, p, name), via_a[h][p]))
        spread(s1, left, h, low_half, 5, 1)
        wait_for(via_b[h], z_recv.at[2, h])
        for p in range(HALF, PPD):
            name = name_of(3, p)
            by_head(s3[h], p, jnp.where((name >> 4) == z, picked(3, h, p, name), via_b[h][p - HALF]))
        spread(s3, right, h, high_half, 6, 3)

    def near_tables():
        wait_for(hv.at[pl.ds(0, 2)], h_sem.at[1])
        send(hv.at[plane(3)], hv.at[plane(3)], h_sem.at[0], h_sem.at[2], at_plane(1))
        to_smem(hv, hs, plane(1), plane(3))

    def far_table():
        wait_for(hv.at[0], h_sem.at[2])
        to_smem(hv, hs, plane(2))

    def gather_new():
        wait_for(na.at[pl.ds(0, 3)], c_recv.at[1])
        wait_for(qa.at[pl.ds(0, 3)], c_recv.at[0])
        for i in (1, 2, 3):
            block = na.at[pl.ds(y * 4, 4)]
            send(block, block, c_send.at[2], c_recv.at[2], at_y(i))
        drain.append((na.at[pl.ds(0, 12)], c_send.at[2]))

    steps = {"o": pass_own, "d": pass_direct, "f": pass_far, "m": pass_merged}
    for step in PLAN:
        if step == "near":
            near_tables()
        elif step == "far":
            far_table()
        elif step == "new":
            gather_new()
        else:
            steps[step[0]](int(step[1]))

    wait_for(mv.at[pl.ds(0, 3)], h_sem.at[4])
    to_smem(mv, ms, 0, 1, 2, 3)

    for i in range(4):
        for g in range(GROUP):
            qm[i, g * 16 : (g + 1) * 16] = qa[i, :, g * HD : (g + 1) * HD]

    def scored(i, keys):
        return lax.dot_general(qm[i], keys, (((1,), (1,)), ((), ())), preferred_element_type=jnp.float32)

    wait_for(na.at[pl.ds(0, 12)], c_recv.at[2])
    new_keys = na[:, 0].reshape(256, HD)
    new_values = na[:, 1].reshape(256, HD)

    def start_rows(i, carry):
        token = (y * 4 + i) * 16 + (lax.broadcasted_iota(jnp.int32, (128, 256), 0) & 15)
        live = lax.broadcasted_iota(jnp.int32, (128, 256), 1) <= token
        scores = jnp.where(live, scored(i, new_keys), MASKED)
        highest = jnp.max(scores, axis=-1, keepdims=True)
        weights = jnp.exp2((scores - highest) * SCALE2)
        top[i] = jnp.broadcast_to(highest, (128, 128))
        tot[i] = jnp.broadcast_to(jnp.sum(weights, axis=-1, keepdims=True), (128, 128))
        acc[i] = jnp.dot(weights.astype(jnp.bfloat16), new_values, preferred_element_type=jnp.float32)
        return carry

    lax.fori_loop(0, 4, start_rows, 0)

    def assemble(h):
        wait_for(own[h].at[pl.ds(0, 3)], z_recv.at[0, h])
        for n in (3, 5):
            wait_for(left[h].at[pl.ds(0, 2)], z_recv.at[n, h])
        for n in (4, 6):
            wait_for(right[h].at[pl.ds(0, 2)], z_recv.at[n, h])
        for i in range(4):
            pages = []
            for p in range(PPD):
                home = ms[i, p, 0] >> 4
                if p < HALF:
                    far = jnp.where(home == plane(1), right[h][i, p], left[h][i, p])
                else:
                    far = jnp.where(home == plane(3), left[h][i, p], right[h][i, p])
                pages.append(jnp.where(home == z, own[h][i, p], far))
            pages = jnp.concatenate(pages, axis=0)
            part = pages[:, 0, :].astype(jnp.float32)
            ka[h][y * 4 + i, 0] = turned(part, past_cos, past_sin).astype(jnp.bfloat16)
            ka[h][y * 4 + i, 1] = pages[:, 1, :]
        for i in (1, 2, 3):
            block = ka[h].at[pl.ds(y * 4, 4)]
            send(block, block, y_send.at[h], y_recv.at[h], at_y(i))
        drain.append((ka[h].at[pl.ds(0, 12)], y_send.at[h]))

    def attend(h, last):
        wait_for(ka[h].at[pl.ds(0, 12)], y_recv.at[h])
        first, tokens = PARTS[h]
        rows = PPD * tokens
        count = 16 * rows
        keys = ka[h][:, 0].reshape(count, HD)
        values = ka[h][:, 1].reshape(count, HD)
        at = lax.broadcasted_iota(jnp.int32, (1, count), 1)
        within = lax.rem(at, rows)
        index = lax.div(at, rows) * (PPD * PAGE) + lax.div(within, tokens) * PAGE + first + lax.rem(within, tokens)
        dead = jnp.where(index < length_ref[0], 0.0, MASKED)

        def add_rows(i, carry):
            scores = scored(i, keys) + dead
            before = top[i][:, 0:1]
            highest = jnp.maximum(before, jnp.max(scores, axis=-1, keepdims=True))
            weights = jnp.exp2((scores - highest) * SCALE2)
            shrink = jnp.exp2((before - highest) * SCALE2)
            top[i] = jnp.broadcast_to(highest, (128, 128))
            tot[i] = tot[i] * shrink + jnp.sum(weights, axis=-1, keepdims=True)
            acc[i] = acc[i] * shrink + jnp.dot(
                weights.astype(jnp.bfloat16), values, preferred_element_type=jnp.float32
            )
            return carry

        if not last:
            lax.fori_loop(0, 4, add_rows, 0, unroll=h >= NZ - 2)
            return
        for step in (1, 2, 3, 0):
            to = lax.rem(low + step, 4)
            add_rows(to, 0)
            result = (acc[to] / tot[to]).astype(jnp.bfloat16)
            for g in range(GROUP):
                os_[to, :, g * HD : (g + 1) * HD] = result[g * 16 : (g + 1) * 16]
            if step:
                send(os_.at[to], oa.at[low], c_send.at[3], c_recv.at[3], at_low(step))
            else:
                oa[low] = os_[low]
        drain.append((os_.at[pl.ds(0, 3)], c_send.at[3]))

    for h in range(NZ):
        assemble(h)
        if h:
            attend(h - 1, False)
    attend(NZ - 1, True)
    wait_for(oa.at[pl.ds(0, 3)], c_recv.at[3])
    for i in range(4):
        out_ref[0, :, i * GROUP * HD : (i + 1) * GROUP * HD] = oa[i]

    for view, sem in drain:
        wait_for(view, sem)


def body(page_store, page_holder, history_length, old_offset, turn_query, turn_key, turn_value):
    middle = np.arange(HD // 2, dtype=np.float32) * np.float32(2.0 / HD)
    freq = (ROPE_BASE ** -middle.astype(np.float64)).astype(np.float32)
    rows = np.zeros((8, HD), np.float32)
    rows[0] = np.concatenate([freq, freq])
    rows[1] = np.concatenate([-np.ones(HD // 2), np.ones(HD // 2)])
    bf16 = jnp.bfloat16
    vmem = pltpu.VMEM
    wide = KVH * HD
    scratch = [vmem((16, tokens, 2, wide), bf16) for _ in range(4) for _, tokens in PARTS]

    def by_part(*shape):
        return [vmem(tuple(n or tokens for n in shape), bf16) for _, tokens in PARTS]

    scratch += by_part(KVH, PPD, 0, 2, HD) * 2 + by_part(PPD, 0, 2, wide) + by_part(KVH, PPD, 0, 2, HD)
    scratch += by_part(HALF, 0, 2, wide) * 2 + by_part(4, PPD, 0, 2, HD) * 3
    scratch += [vmem((16, 2, PPD * tokens, HD), bf16) for _, tokens in PARTS]
    scratch += [
        vmem((4, 2, 16, HD), bf16),
        vmem((16, 2, 16, HD), bf16),
        vmem((4, 16, GROUP * HD), bf16),
        vmem((4, 16, GROUP * HD), bf16),
        vmem((4, 128, HD), bf16),
        vmem((4, 16, GROUP * HD), bf16),
        vmem((4, 16, GROUP * HD), bf16),
        vmem((4, PPD, 128), jnp.int32),
        pltpu.SMEM((4, PPD, 128), jnp.int32),
        vmem((4, PPD, 128), jnp.int32),
        pltpu.SMEM((4, PPD, 128), jnp.int32),
        vmem((4, 128, HD), jnp.float32),
        vmem((4, 128, 128), jnp.float32),
        vmem((4, 128, 128), jnp.float32),
        pltpu.SMEM((1, PPD), jnp.int32),
        pltpu.SMEM((1,), jnp.int32),
        pltpu.SMEM((1,), jnp.int32),
        vmem((8, HD), jnp.float32),
        vmem(turn_query.shape, bf16),
        vmem(turn_key.shape, bf16),
        vmem(turn_value.shape, bf16),
        pltpu.SemaphoreType.DMA((4, NZ)),
        pltpu.SemaphoreType.DMA((4, NZ)),
        pltpu.SemaphoreType.DMA((7, NZ)),
        pltpu.SemaphoreType.DMA((7, NZ)),
        pltpu.SemaphoreType.DMA((NZ,)),
        pltpu.SemaphoreType.DMA((NZ,)),
        pltpu.SemaphoreType.DMA((4,)),
        pltpu.SemaphoreType.DMA((4,)),
        pltpu.SemaphoreType.DMA((5,)),
        pltpu.SemaphoreType.DMA((11,)),
    ]
    there = pl.BlockSpec(memory_space=pltpu.HBM)
    return pl.pallas_call(
        kernel,
        out_shape=jax.ShapeDtypeStruct(turn_query.shape, bf16),
        in_specs=[there] * 8,
        out_specs=pl.BlockSpec(memory_space=pltpu.VMEM),
        scratch_shapes=scratch,
        compiler_params=pltpu.CompilerParams(
            collective_id=0, has_side_effects=True, vmem_limit_bytes=64 * 1024 * 1024 - 65536
        ),
        name="restore_attend",
    )(page_holder.reshape(1, PPD), history_length, old_offset, jnp.asarray(rows), page_store, turn_query, turn_key, turn_value)


def solution(mesh):
    placed = (
        P("sess", "ctx", None, None, None, None, None),
        P("sess", "ctx", None),
        P("sess"),
        P("sess"),
        P("sess", "ctx", None),
        P("sess", "ctx", None),
        P("sess", "ctx", None),
    )
    return jax.shard_map(
        body, mesh=mesh, in_specs=placed, out_specs=P("sess", "ctx", None), check_vma=False
    )
```
